32 devices in a mesh: groups: 2 (over y), dp: 16 (over z, x, core).
Axes of the slice: x: 2, y: 2, z: 4, core: 2. Of those that a mesh axis runs over, the one named last changes fastest.
Arguments:
- merger_input: bfloat16 [3072, 2304], P(('groups', 'dp')), parts along dimension 0, may hold values from -6 to 6
- merger_weight: bfloat16 [2304, 2048], P('dp'), may hold values from -0.125 to 0.125
- merger_bias: float32 [2048], replicated, may hold values from -3 to 3
- norm_gain: float32 [2048], replicated, may hold values from 0.5 to 1.5
- gate_weight: bfloat16 [16, 2048, 768], P('dp'), may hold values from -0.125 to 0.125
- up_weight: bfloat16 [16, 2048, 768], P('dp'), may hold values from -0.125 to 0.125
- down_weight: bfloat16 [16, 768, 2048], P('dp'), may hold values from -0.21875 to 0.21875
- expert_ids: int32 [3072, 8], P(('groups', 'dp')), parts along dimension 0, may hold values from 0 to 15, all different within a row; in each aligned block of 96 rows (0 to 95, 96 to 191, ...) at most 72 rows name the same one
- combine_ints: int32 [3072, 8], P(('groups', 'dp')), parts along dimension 0, may hold values from 1 to 16
Outputs:
- mixed: bfloat16 [3072, 2048], P(('groups', 'dp')), parts along dimension 0
The draws below stay inside these ranges and needn't reach their ends.
There are 2 independent parts, one for each index of `groups`. The reference program is written for one: setup_inputs(seed, part) draws one part's arguments, and reference() takes and returns one part's arrays. A program takes and returns all parts, laid end to end along the dimension named above; an argument that names none is the same for every part. Nothing has to cross between parts.
Inputs may be any that keep to these rules, and one draw needn't show every extreme that they name: `expert_ids`: each row names 8 different experts; in the rows of one device no expert is named more than 72 times, and that many is reached.
All inputs are finite; a program needn't handle non-finite values.
Results may differ from the reference program's by a relative error of at most 0.0051.
Values may be sent and summed in bfloat16 or wider, within the bound.
A program may use at most 128 MiB of HBM per device.

```python
import math
import jax
import jax.numpy as jnp
import numpy as np
from jax import lax

D = 2048
EXPERT_HIDDEN = 768
MERGE = 2304
TOP = 8
ROWS_DEV = 96
EXPERTS = 16
ROWS = 1536
CAP = 72
N_DP = 16


def plant(drawn, own_key, low, largest):
    longest = drawn.shape.index(max(drawn.shape))
    spots = []
    for shift in (0, 1):
        where = [jax.random.randint(jax.random.fold_in(own_key, axis), (), 0, length) for axis, length in enumerate(drawn.shape)]
        where[longest] = (where[longest] + shift) % drawn.shape[longest]
        spots.append(tuple(where))
    return drawn.at[spots[0]].set(low).at[spots[1]].set(largest)


def block_scale(own_key, extent, shards, least, top_value):
    def one(dim, blocks):
        steps = jax.random.uniform(jax.random.fold_in(jax.random.fold_in(own_key, 6), dim), (blocks,), jnp.float32, least / len(shards), top_value / len(shards))
        return jnp.repeat(jnp.exp(steps), extent[dim] // blocks).reshape((-1,) + (1,) * (len(extent) - dim - 1))

    gain = one(*shards[0])
    for cut in shards[1:]:
        gain = gain * one(*cut)
    return gain


def deal_out(rng, own, number, rows, amount, top, most, lean):
    ranking = jax.random.permutation(rng, amount)
    heavy_load, usual = shares(amount, rows * top, most, lean, True), shares(amount, rows * top, most, lean, False)
    places = jnp.arange(amount)

    def named(sizes, offset_by):
        used = int((sizes > 0).sum())
        fixed = max(1, used // 4)
        moved = fixed + (places - fixed + offset_by * (used - fixed)) % max(1, amount - fixed)
        return jnp.zeros((amount,), jnp.int32).at[ranking[jnp.where(places < fixed, places, moved)]].set(jnp.asarray(sizes, jnp.int32))

    sizes = jnp.where(number % 4 == 0, named(heavy_load, number // 4), named(usual, number - number // 4 - 1))
    mixed = jax.random.permutation(jax.random.fold_in(own, 3), amount)
    giver, sink = mixed[0:amount // 2 * 2:2], mixed[1:amount // 2 * 2:2]
    slack = jnp.minimum(sizes[giver] - 1, most - sizes[sink]) // 2
    slack = jnp.where((giver == ranking[0]) | (sink == ranking[0]) | (sizes[sink] == 0), 0, jnp.maximum(slack, 0))
    moved = jax.random.randint(jax.random.fold_in(own, 4), (amount // 2,), 0, 1 << 20) % (slack + 1)
    sizes = sizes.at[giver].add(-moved).at[sink].add(moved)
    items = jnp.searchsorted(jnp.cumsum(sizes), jnp.arange(rows * top), side="right").astype(jnp.int32)
    table = items.reshape(top, rows).T
    table = table[jax.random.permutation(jax.random.fold_in(own, 1), rows)]
    offset_by = jax.random.randint(jax.random.fold_in(own, 2), (rows, 1), 0, top)
    return jnp.take_along_axis(table, (jnp.arange(top)[None, :] + offset_by) % top, axis=1)


def shares(number_of, total, reach, lean, full):
    loads = [(1 << 20) // math.isqrt(standing ** lean) + 1 for standing in range(1, number_of + 1)]
    largest = reach if full else min(reach, max(-(-total // number_of), total * loads[0] // sum(loads)))
    least = 1 if total - largest >= number_of - 1 else 0
    given, rest = [largest] + [least] * (number_of - 1), total - largest - least * (number_of - 1)
    while rest > 0:
        candidates = [i for i in range(1, number_of) if given[i] < largest] or [i for i in range(1, number_of) if given[i] < reach]
        whole, remaining = sum([loads[i] for i in candidates]), rest
        for i in candidates:
            addition = min(reach - given[i], max(1, remaining * loads[i] // whole), rest)
            given[i] = given[i] + addition
            rest = rest - addition
    return np.array(given)


def normal_values(rng, dims, deviation, reach, shards=(), kind=jnp.bfloat16):
    array = deviation * jax.random.normal(rng, dims, jnp.float32)
    if shards:
        array = array * block_scale(rng, dims, shards, -0.22, 0.18)
    return jnp.clip(array, -reach, reach).astype(kind)


def setup_inputs(seed: int = 0, part: int = 0) -> dict:
    arg_keys = jax.random.split(jax.random.key(seed), 10)
    part_keys = jax.random.split(jax.random.fold_in(arg_keys[9], part), 10)
    merger_input = normal_values(part_keys[0], (ROWS, MERGE), 1.0, 6.0, ((0, 16),))
    merger_weight = normal_values(arg_keys[1], (MERGE, D), MERGE ** -0.5, 0.125, ((0, 16),))
    merger_bias = normal_values(arg_keys[2], (D,), 0.5, 3.0, (), jnp.float32)
    norm_gain = jnp.clip(jax.random.uniform(arg_keys[3], (D,), jnp.float32, 0.5, 1.5), 0.5, 1.5)
    gate_weight = normal_values(arg_keys[4], (EXPERTS, D, EXPERT_HIDDEN), D ** -0.5, 0.125, ((0, 16),))
    up_weight = normal_values(arg_keys[5], (EXPERTS, D, EXPERT_HIDDEN), D ** -0.5, 0.125, ((0, 16),))
    down_weight = normal_values(arg_keys[6], (EXPERTS, EXPERT_HIDDEN, D), EXPERT_HIDDEN ** -0.5, 0.21875, ((0, 16),))
    expert_ids_keys = jax.random.split(jax.random.fold_in(part_keys[7], 1), ROWS // ROWS_DEV)
    expert_ids_turns = jax.random.permutation(jax.random.fold_in(part_keys[7], 3), ROWS // ROWS_DEV)
    expert_ids = jax.vmap(lambda own, number: deal_out(jax.random.fold_in(part_keys[7], 2), own, number, ROWS_DEV, EXPERTS, TOP, CAP, 2))(expert_ids_keys, expert_ids_turns).reshape((ROWS, TOP))
    combine_ints = plant(jax.random.randint(part_keys[8], (ROWS, TOP), 1, 17), jax.random.fold_in(part_keys[8], 1), 1, 16).astype(jnp.int32)
    return dict(merger_input=merger_input, merger_weight=merger_weight, merger_bias=merger_bias, norm_gain=norm_gain, gate_weight=gate_weight, up_weight=up_weight, down_weight=down_weight, expert_ids=expert_ids, combine_ints=combine_ints)


def reference(merger_input, merger_weight, merger_bias, norm_gain, gate_weight, up_weight, down_weight, expert_ids, combine_ints):
    act = jax.nn.gelu(merger_input.astype(jnp.float32), approximate=False).astype(jnp.bfloat16)
    merged = jnp.dot(act, merger_weight, preferred_element_type=jnp.float32) + merger_bias
    scale = lax.rsqrt(lax.optimization_barrier(jnp.mean(merged * merged, axis=1, keepdims=True)) + 1e-06)
    normed = (merged * scale * norm_gain).astype(jnp.bfloat16)
    onehot = (expert_ids[:, :, None] == jnp.arange(EXPERTS, dtype=jnp.int32)[None, None, :]).astype(jnp.int32)
    blocks = onehot.reshape(N_DP, ROWS_DEV * TOP, EXPERTS)
    before = jnp.cumsum(blocks, axis=1) - blocks
    position = lax.optimization_barrier(jnp.sum(before * blocks, axis=2)).reshape(ROWS, TOP)
    block_id = (jnp.arange(ROWS, dtype=jnp.int32) // ROWS_DEV)[:, None]
    slot = (block_id * CAP + position).astype(jnp.int32)
    row_index = jnp.broadcast_to(jnp.arange(ROWS, dtype=jnp.int32)[:, None], (ROWS, TOP))
    table = jnp.full((EXPERTS, N_DP * CAP), ROWS, jnp.int32).at[expert_ids, slot].set(row_index)
    padded = jnp.concatenate([normed, jnp.zeros((1, D), jnp.bfloat16)], axis=0)

    def serve(expert):
        inputs = padded[table[expert]].astype(jnp.float32)
        gate = jnp.dot(inputs, gate_weight[expert].astype(jnp.float32))
        up = jnp.dot(inputs, up_weight[expert].astype(jnp.float32))
        hidden = (jax.nn.silu(gate) * up).astype(jnp.bfloat16)
        return jnp.dot(hidden.astype(jnp.float32), down_weight[expert].astype(jnp.float32)).astype(jnp.bfloat16)
    results = lax.map(serve, jnp.arange(EXPERTS, dtype=jnp.int32))
    picked = results[expert_ids, slot]
    counts = combine_ints.astype(jnp.float32)
    weights = counts / lax.optimization_barrier(jnp.sum(counts, axis=1, keepdims=True))
    combined = lax.optimization_barrier(jnp.sum(weights[:, :, None] * picked.astype(jnp.float32), axis=1))
    return (merged + combined).astype(jnp.bfloat16)
```

```python
import functools

import jax
import jax.numpy as jnp
from jax import lax
from jax.experimental import pallas as pl
from jax.experimental.pallas import tpu as pltpu
from jax.sharding import PartitionSpec as P

LANES = 128
VMEM_BYTES = 60 << 20
F32, BF16 = jnp.float32, jnp.bfloat16


def run_experts(received, gate_weight, up_weight, down_weight, ndevices):
    local = gate_weight.shape[0]
    slots = received.shape[1]
    width = received.shape[2]
    inputs = received.reshape(ndevices, local, slots, width)
    gate = jnp.einsum("jlcd,ldh->jlch", inputs, gate_weight, preferred_element_type=F32)
    up = jnp.einsum("jlcd,ldh->jlch", inputs, up_weight, preferred_element_type=F32)
    hidden = (jax.nn.silu(gate) * up).astype(BF16)
    output = jnp.einsum("jlch,lhd->jlcd", hidden, down_weight, preferred_element_type=F32)
    return output.astype(BF16).reshape(ndevices * local, slots, width)


def routed_shards(
    act,
    merger_weight,
    merger_bias,
    norm_gain,
    gate_weight,
    up_weight,
    down_weight,
    expert_ids,
    combine_ints,
):
    ndevices = lax.axis_size("dp")
    rows = act.shape[0]
    width = merger_weight.shape[1]
    choose = expert_ids.shape[1]
    experts_all = gate_weight.shape[0] * ndevices
    capacity = (3 * rows * choose + 2 * ndevices - 1) // (2 * ndevices)
    merged = jnp.dot(
        act,
        lax.all_gather(merger_weight, "dp", axis=0, tiled=True),
        preferred_element_type=F32,
    )
    merged = merged + merger_bias
    scale = lax.rsqrt(jnp.mean(merged * merged, axis=1, keepdims=True) + 1e-06)
    normed = (merged * scale * norm_gain).astype(BF16)
    pairs = rows * choose
    flat = expert_ids.reshape(pairs)
    earlier = jnp.arange(pairs)[:, None] > jnp.arange(pairs)[None, :]
    position = jnp.sum((earlier & (flat[:, None] == flat[None, :])).astype(jnp.int32), axis=1)
    slot_flat = flat * capacity + position
    repeated = jnp.repeat(normed, choose, axis=0)
    outgoing = jnp.zeros((experts_all * capacity, width), BF16).at[slot_flat].set(repeated)
    outgoing = outgoing.reshape(experts_all, capacity, width)
    received = lax.all_to_all(outgoing, "dp", split_axis=0, concat_axis=0, tiled=True)
    served = run_experts(received, gate_weight, up_weight, down_weight, ndevices)
    returned = lax.all_to_all(served, "dp", split_axis=0, concat_axis=0, tiled=True)
    returned = returned.reshape(experts_all * capacity, width)
    picked = returned[slot_flat].reshape(rows, choose, width)
    counts = combine_ints.astype(F32)
    weights = counts / jnp.sum(counts, axis=1, keepdims=True)
    combined = jnp.sum(weights[:, :, None] * picked.astype(F32), axis=1)
    return (merged + combined).astype(BF16)


def fused_kernel(
    n,
    act_ref,
    counts_ref,
    bias_ref,
    gain_ref,
    weight_hbm,
    gate_hbm,
    up_hbm,
    down_hbm,
    out_ref,
    wbuf,
    xbuf,
    part,
    sib,
    from_left,
    from_right,
    gate_v,
    up_v,
    down_v,
    merged,
    hid,
    local_sem,
    w_sems,
    w_sib,
    x_sems,
    x_sib,
    r_sems,
    r_sib,
):
    chips = n // 2
    half = chips // 2
    depth, width = weight_hbm.shape
    rows = counts_ref.shape[0]
    hidden = gate_v.shape[1]
    me = lax.axis_index("dp")
    core, chip = me % 2, me // 2
    x, z = chip % 2, chip // 2
    pos = z * (1 - x) + (chips - 1 - z) * x

    def chip_at(p):
        p = lax.rem(p + chips, chips)
        xx = p // half
        return (p * (1 - xx) + (chips - 1 - p) * xx) * 2 + xx

    right = chip_at(pos + 1) * 2 + core
    left = chip_at(pos - 1) * 2 + core
    sibling = chip * 2 + 1 - core
    sent = []

    def remote(src, dst, sems, where, device):
        return pltpu.make_async_remote_copy(
            src_ref=src,
            dst_ref=dst,
            send_sem=sems.at[(0, *where)],
            recv_sem=sems.at[(1, *where)],
            device_id={"dp": device},
            device_id_type=pl.DeviceIdType.MESH,
        )

    def start(copy):
        copy.start()
        sent.append(copy)

    loads = [
        pltpu.make_async_copy(
            weight_hbm, wbuf.at[chip, pl.ds(core * depth, depth), :], local_sem.at[0]
        ),
        pltpu.make_async_copy(gate_hbm.at[0], gate_v, local_sem.at[1]),
        pltpu.make_async_copy(up_hbm.at[0], up_v, local_sem.at[2]),
        pltpu.make_async_copy(down_hbm.at[0], down_v, local_sem.at[3]),
    ]
    loads[0].start()
    barrier = pltpu.get_barrier_semaphore()
    for device in (left, right, sibling):
        pl.semaphore_signal(
            barrier, inc=1, device_id={"dp": device}, device_id_type=pl.DeviceIdType.MESH
        )
    pl.semaphore_wait(barrier, 3)
    loads[0].wait()

    def gather(buf, tall, sems, sib_sems, work, after_start):
        columns = buf.shape[2]
        cut = width // 2
        spans = ((0, cut), (cut, columns - cut))

        def piece(at, c, q):
            lo, size = spans[q]
            return buf.at[at, pl.ds(c * tall, tall), pl.ds(lo, size)]

        def ring(way, h, q):
            sign = 1 if way == 0 else -1
            at = chip_at(pos - sign * (h - 1))
            return remote(
                piece(at, core, q), piece(at, core, q), sems, (way, h - 1, q),
                right if way == 0 else left,
            )

        def across(at, i, q):
            return remote(piece(at, core, q), piece(at, core, q), sib_sems, (i, q), sibling)

        def goes(way, h, q):
            return h < half or (h == half and q == way)

        def number(way, h):
            return 0 if h == 0 else 2 * half - 1 if h == half else h + way * (half - 1)

        def arrived(at, i):
            for q in range(2):
                lo, size = spans[q]
                ref = buf.at[at, pl.ds((1 - core) * tall, tall), pl.ds(lo, size)]
                remote(ref, ref, sib_sems, (i, q), sibling).wait_recv()

        for q in range(2):
            for way in range(2):
                start(ring(way, 1, q))
        for q in range(2):
            start(across(chip, 0, q))
        after_start()
        for h in range(1, half + 1):
            for q in range(2):
                for way in range(2):
                    if not goes(way, h, q):
                        continue
                    sign = 1 if way == 0 else -1
                    at = chip_at(pos - sign * h)
                    ref = piece(at, core, q)
                    remote(ref, ref, sems, (way, h - 1, q), left).wait_recv()
                    if goes(way, h + 1, q):
                        start(ring(way, h + 1, q))
                    start(across(at, number(way, h), q))
                if h == 1:
                    if q == 0:
                        arrived(chip, 0)
                        work(chip, 0)
                else:
                    at = chip_at(pos - (h - 1) if q == 0 else pos + (h - 1))
                    arrived(at, number(q, h - 1))
                    work(at, number(q, h - 1))
        arrived(chip_at(pos + half), 2 * half - 1)

    tile = 512

    merged[...] = jnp.broadcast_to(bias_ref[...], merged.shape)

    def merge(at, i):
        @pl.loop(0, width // tile)
        def _(j):
            cols = pl.ds(pl.multiple_of(j * tile, tile), tile)
            merged[:, cols] += jnp.dot(act_ref[at], wbuf[at, :, cols], preferred_element_type=F32)

    def load_experts():
        for copy in loads[1:]:
            copy.start()

    gather(wbuf, depth, w_sems, w_sib, merge, load_experts)
    far = chip_at(pos + half)
    merge(far, 0)

    value = merged[...]
    scale = lax.rsqrt(jnp.mean(value * value, axis=1, keepdims=True) + 1e-06)
    mine = pl.ds(core * rows, rows)
    xbuf[chip, mine, pl.ds(0, width)] = (value * scale * gain_ref[...]).astype(BF16)
    xbuf[chip, mine, pl.ds(width, LANES)] = counts_ref[...]

    theirs = pl.ds((1 - core) * rows, rows)

    def swap(at, i):
        return remote(part.at[at, theirs, :], sib.at[at], r_sib, (i,), sibling)

    hid_tile = 256

    def expert(at, i):
        @pl.loop(0, hidden // hid_tile)
        def _(j):
            cols = pl.ds(pl.multiple_of(j * hid_tile, hid_tile), hid_tile)
            block = xbuf[at, :, pl.ds(0, width)]
            gate = jnp.dot(block, gate_v[:, cols], preferred_element_type=F32)
            up = jnp.dot(block, up_v[:, cols], preferred_element_type=F32)
            hid[:, cols] = (jax.nn.silu(gate) * up).astype(BF16)

        counts = xbuf[at, :, pl.ds(width, LANES)].astype(F32)
        lane = lax.broadcasted_iota(jnp.int32, counts.shape, 1)
        factor = jnp.sum(jnp.where(lane == me, counts, 0.0), axis=1, keepdims=True)

        @pl.loop(0, width // tile)
        def _(j):
            cols = pl.ds(pl.multiple_of(j * tile, tile), tile)
            result = jnp.dot(hid[...], down_v[:, cols], preferred_element_type=F32).astype(BF16)
            part[at, :, cols] = (result.astype(F32) * factor).astype(BF16)

        start(swap(at, i))

    def wait_experts():
        for copy in loads[1:]:
            copy.wait()

    gather(xbuf, rows, x_sems, x_sib, expert, wait_experts)

    cut = width // 2

    def span(q):
        return pl.ds(q * cut, cut)

    def landing(way, k):
        return (from_left if way == 0 else from_right).at[k - 1]

    def returned(way, k, q):
        dist = half + 1 - k
        at = chip_at(pos + dist if way == 0 else pos - dist)
        return remote(
            part.at[at, mine, span(q)],
            landing(way, k).at[:, span(q)],
            r_sems,
            (way, k - 1, q),
            right if way == 0 else left,
        )

    def swapped(at, i):
        ref = sib.at[at]
        remote(ref, ref, r_sib, (i,), sibling).wait_recv()

    def landed(way, k, q):
        ref = landing(way, k).at[:, span(q)]
        remote(ref, ref, r_sems, (way, k - 1, q), left).wait_recv()

    def both(at, q):
        return part[at, mine, span(q)].astype(F32) + sib[at, :, span(q)].astype(F32)

    def send(way, k, q, more):
        dist = half + 1 - k
        at = chip_at(pos + dist if way == 0 else pos - dist)
        total = both(at, q)
        if more:
            landed(way, k - 1, q)
            total = total + landing(way, k - 1)[:, span(q)].astype(F32)
        part[at, mine, span(q)] = total.astype(BF16)
        start(returned(way, k, q))

    for way in range(2):
        d = half - 1
        at = chip_at(pos + d if way == 0 else pos - d)
        swapped(at, d + (1 - way) * (half - 1))
        send(way, 2, 1 - way, False)
    expert(far, 2 * half - 1)
    swapped(far, 2 * half - 1)
    for way in range(2):
        send(way, 1, way, False)
    for k in range(2, half + 1):
        dist = half + 1 - k
        if k > 2:
            for way in range(2):
                at = chip_at(pos + dist if way == 0 else pos - dist)
                swapped(at, dist + (1 - way) * (half - 1))
            for way in range(2):
                send(way, k, 1 - way, True)
        for way in range(2):
            send(way, k, way, True)
    swapped(chip, 0)
    inverse = 1.0 / jnp.sum(counts_ref[...].astype(F32), axis=1, keepdims=True)
    for q in range(2):
        total = both(chip, q)
        for way in range(2):
            landed(way, half, q)
            total = total + landing(way, half)[:, span(q)].astype(F32)
        out_ref[:, span(q)] = (merged[:, span(q)] + total * inverse).astype(BF16)
    for copy in sent:
        copy.wait_send()


def fused_shards(
    act, merger_weight, merger_bias, norm_gain, gate_weight, up_weight, down_weight, counts
):
    n = lax.axis_size("dp")
    chips, half = n // 2, n // 4
    rows = act.shape[0]
    depth, width = merger_weight.shape
    hidden = gate_weight.shape[2]
    by_chip = act.reshape(rows, chips, 2 * depth).transpose(1, 0, 2)
    vmem = pl.BlockSpec(memory_space=pltpu.VMEM)
    hbm = pl.BlockSpec(memory_space=pl.ANY)
    dma = pltpu.SemaphoreType.DMA
    return pl.pallas_call(
        functools.partial(fused_kernel, n),
        out_shape=jax.ShapeDtypeStruct((rows, width), BF16),
        in_specs=[vmem] * 4 + [hbm] * 4,
        out_specs=vmem,
        scratch_shapes=[
            pltpu.VMEM((chips, 2 * depth, width), BF16),
            pltpu.VMEM((chips, 2 * rows, width + LANES), BF16),
            pltpu.VMEM((chips, 2 * rows, width), BF16),
            pltpu.VMEM((chips, rows, width), BF16),
            pltpu.VMEM((half, rows, width), BF16),
            pltpu.VMEM((half, rows, width), BF16),
            pltpu.VMEM((width, hidden), BF16),
            pltpu.VMEM((width, hidden), BF16),
            pltpu.VMEM((hidden, width), BF16),
            pltpu.VMEM((rows, width), F32),
            pltpu.VMEM((2 * rows, hidden), BF16),
            dma((4,)),
            dma((2, 2, half, 2)),
            dma((2, chips, 2)),
            dma((2, 2, half, 2)),
            dma((2, chips, 2)),
            dma((2, 2, half, 2)),
            dma((2, chips)),
        ],
        compiler_params=pltpu.CompilerParams(
            collective_id=0, has_side_effects=True, vmem_limit_bytes=VMEM_BYTES
        ),
    )(
        by_chip,
        counts,
        merger_bias[None, :],
        norm_gain[None, :],
        merger_weight,
        gate_weight,
        up_weight,
        down_weight,
    )


def fits(n, rows, depth, width, hidden, local):
    if n % 4 or n < 8 or n > LANES or local != 1 or rows % 16 or depth % 16:
        return False
    if width % 512 or hidden % 256:
        return False
    gathered = n * (depth * width + rows * (width + LANES))
    sums = n * rows * width * 2 + n * rows * width // 2
    rest = 3 * width * hidden + 2 * rows * (hidden + width) + n * rows * depth
    return 2 * (gathered + sums + rest) < VMEM_BYTES - (8 << 20)


def shards(
    merger_input,
    merger_weight,
    merger_bias,
    norm_gain,
    gate_weight,
    up_weight,
    down_weight,
    expert_ids,
    combine_ints,
):
    n = lax.axis_size("dp")
    rows = merger_input.shape[0]
    depth, width = merger_weight.shape
    local, _, hidden = gate_weight.shape
    act = jax.nn.gelu(merger_input.astype(F32), approximate=False).astype(BF16)
    weights = (merger_weight, merger_bias, norm_gain, gate_weight, up_weight, down_weight)
    if not fits(n, rows, depth, width, hidden, local):
        return routed_shards(act, *weights, expert_ids, combine_ints)
    named = expert_ids[:, :, None] == jnp.arange(LANES, dtype=jnp.int32)
    counts = jnp.sum(jnp.where(named, combine_ints[:, :, None], 0), axis=1).astype(BF16)
    return fused_shards(act, *weights, counts)


def solution(mesh):
    placed = (
        P(("groups", "dp"), None),
        P("dp", None),
        P(),
        P(),
        P("dp", None, None),
        P("dp", None, None),
        P("dp", None, None),
        P(("groups", "dp"), None),
        P(("groups", "dp"), None),
    )
    return jax.shard_map(
        shards, mesh=mesh, in_specs=placed, out_specs=P(("groups", "dp"), None), check_vma=False
    )
```

```python
import functools

import jax
import jax.numpy as jnp
from jax import lax
from jax.experimental import pallas as pl
from jax.experimental.pallas import tpu as pltpu
from jax.sharding import PartitionSpec as P

LANES = 128
VMEM_BYTES = 60 << 20
W_PLAN = ((5, 1, 1), (6, 0, 0))
X_PLAN = ((8, 0, 0), (8, 1, 0))
F32, BF16 = jnp.float32, jnp.bfloat16


def run_experts(received, gate_weight, up_weight, down_weight, ndevices):
    local = gate_weight.shape[0]
    slots = received.shape[1]
    width = received.shape[2]
    inputs = received.reshape(ndevices, local, slots, width)
    gate = jnp.einsum("jlcd,ldh->jlch", inputs, gate_weight, preferred_element_type=F32)
    up = jnp.einsum("jlcd,ldh->jlch", inputs, up_weight, preferred_element_type=F32)
    hidden = (jax.nn.silu(gate) * up).astype(BF16)
    output = jnp.einsum("jlch,lhd->jlcd", hidden, down_weight, preferred_element_type=F32)
    return output.astype(BF16).reshape(ndevices * local, slots, width)


def routed_shards(
    act,
    merger_weight,
    merger_bias,
    norm_gain,
    gate_weight,
    up_weight,
    down_weight,
    expert_ids,
    combine_ints,
):
    ndevices = lax.axis_size("dp")
    rows = act.shape[0]
    width = merger_weight.shape[1]
    choose = expert_ids.shape[1]
    experts_all = gate_weight.shape[0] * ndevices
    capacity = (3 * rows * choose + 2 * ndevices - 1) // (2 * ndevices)
    merged = jnp.dot(
        act,
        lax.all_gather(merger_weight, "dp", axis=0, tiled=True),
        preferred_element_type=F32,
    )
    merged = merged + merger_bias
    scale = lax.rsqrt(jnp.mean(merged * merged, axis=1, keepdims=True) + 1e-06)
    normed = (merged * scale * norm_gain).astype(BF16)
    pairs = rows * choose
    flat = expert_ids.reshape(pairs)
    earlier = jnp.arange(pairs)[:, None] > jnp.arange(pairs)[None, :]
    position = jnp.sum((earlier & (flat[:, None] == flat[None, :])).astype(jnp.int32), axis=1)
    slot_flat = flat * capacity + position
    repeated = jnp.repeat(normed, choose, axis=0)
    outgoing = jnp.zeros((experts_all * capacity, width), BF16).at[slot_flat].set(repeated)
    outgoing = outgoing.reshape(experts_all, capacity, width)
    received = lax.all_to_all(outgoing, "dp", split_axis=0, concat_axis=0, tiled=True)
    served = run_experts(received, gate_weight, up_weight, down_weight, ndevices)
    returned = lax.all_to_all(served, "dp", split_axis=0, concat_axis=0, tiled=True)
    returned = returned.reshape(experts_all * capacity, width)
    picked = returned[slot_flat].reshape(rows, choose, width)
    counts = combine_ints.astype(F32)
    weights = counts / jnp.sum(counts, axis=1, keepdims=True)
    combined = jnp.sum(weights[:, :, None] * picked.astype(F32), axis=1)
    return (merged + combined).astype(BF16)


def cut_up(plan, width, group):
    unit = width // 16
    split = unit * sum(size for size, _, shared in plan if shared)
    bases = (0, width - 2 * split + group * split, width - 2 * split + (1 - group) * split)
    at, spans, twins = [0, 0], [], []
    for size, way, shared in plan:
        lo = at[shared] * unit
        spans.append((bases[shared] + lo, size * unit, way, shared))
        if shared:
            twins.append((bases[2] + lo, size * unit, way, shared))
        at[shared] += size
    return spans, twins


def fused_kernel(
    n,
    paired,
    input_ref,
    ids_ref,
    ints_ref,
    bias_ref,
    gain_ref,
    weight_hbm,
    gate_hbm,
    up_hbm,
    down_hbm,
    out_ref,
    act,
    cbuf,
    wbuf,
    xbuf,
    part,
    sib,
    from_left,
    from_right,
    gate_v,
    up_v,
    down_v,
    merged,
    hid,
    local_sem,
    w_sems,
    w_sib,
    w_twin,
    x_sems,
    x_sib,
    r_sems,
    r_sib,
):
    chips = n // 2
    half = chips // 2
    depth, width = weight_hbm.shape
    hidden = gate_v.shape[1]
    group = lax.axis_index("groups")
    me = lax.axis_index("dp")
    core, chip = me % 2, me // 2
    x, z = chip % 2, chip // 2
    pos = z * (1 - x) + (chips - 1 - z) * x

    def chip_at(p):
        p = lax.rem(p + chips, chips)
        xx = p // half
        return (p * (1 - xx) + (chips - 1 - p) * xx) * 2 + xx

    right = chip_at(pos + 1) * 2 + core
    left = chip_at(pos - 1) * 2 + core
    sibling = chip * 2 + 1 - core
    sent = []

    def remote(src, dst, sems, where, device_id):
        return pltpu.make_async_remote_copy(
            src_ref=src,
            dst_ref=dst,
            send_sem=sems.at[(0, *where)],
            recv_sem=sems.at[(1, *where)],
            device_id=device_id,
            device_id_type=pl.DeviceIdType.MESH,
        )

    def start(copy):
        copy.start()
        sent.append(copy)

    loads = [
        pltpu.make_async_copy(
            weight_hbm, wbuf.at[chip, pl.ds(core * depth, depth), :], local_sem.at[0]
        ),
        pltpu.make_async_copy(gate_hbm.at[0], gate_v, local_sem.at[1]),
        pltpu.make_async_copy(up_hbm.at[0], up_v, local_sem.at[2]),
        pltpu.make_async_copy(down_hbm.at[0], down_v, local_sem.at[3]),
    ]
    loads[0].start()
    rows = ids_ref.shape[1]
    named = lax.broadcasted_iota(jnp.int32, (n, rows), 0)
    total = jnp.zeros((n, rows), jnp.int32)
    for k in range(ids_ref.shape[0]):
        total += jnp.where(named == ids_ref[k : k + 1, :], ints_ref[k : k + 1, :], 0)
    counts = jnp.concatenate([total.astype(F32), jnp.zeros((n, LANES - rows), F32)], axis=1)
    cbuf[chip, pl.ds(core * n, n), :] = counts.astype(BF16)
    barrier = pltpu.get_barrier_semaphore()
    others = [{"dp": left}, {"dp": right}, {"dp": sibling}] + ([{"groups": 1 - group}] if paired else [])
    for device_id in others:
        pl.semaphore_signal(
            barrier, inc=1, device_id=device_id, device_id_type=pl.DeviceIdType.MESH
        )
    pl.semaphore_wait(barrier, len(others))
    loads[0].wait()

    def gather(buf, tall, spans, twins, sems, sib_sems, twin_sems, work, after_start):
        count = len(spans)
        shared = [q for q in range(count) if spans[q][3]]

        def piece(at, c, lo, size):
            if lo is None:
                return cbuf.at[at, pl.ds(c * n, n), :]
            return buf.at[at, pl.ds(c * tall, tall), pl.ds(lo, size)]

        def ring(way, h, q):
            sign = 1 if way == 0 else -1
            ref = piece(chip_at(pos - sign * (h - 1)), core, *spans[q][:2])
            return remote(ref, ref, sems, (way, h - 1, q), {"dp": right if way == 0 else left})

        def across(at, i, q):
            ref = piece(at, core, *(spans + twins)[q][:2])
            return remote(ref, ref, sib_sems, (i, q), {"dp": sibling})

        def over(at, i, s):
            ref = piece(at, core, *spans[shared[s]][:2])
            return remote(ref, ref, twin_sems, (i, s), {"groups": 1 - group})

        def goes(way, h, q):
            return h < half or (h == half and spans[q][2] == way)

        def number(way, h):
            return 0 if h == 0 else 2 * half - 1 if h == half else h + way * (half - 1)

        def blocks(h):
            if h == 0:
                return [(chip, 0)]
            if h == half:
                return [(chip_at(pos + half), 2 * half - 1)]
            return [(chip_at(pos - h), number(0, h)), (chip_at(pos + h), number(1, h))]

        def from_twin(h):
            for s in range(len(shared)):
                for at, i in blocks(h):
                    ref = piece(at, core, *twins[s][:2])
                    remote(ref, ref, twin_sems, (i, s), {"groups": 1 - group}).wait_recv()
                    start(across(at, i, count + s))

        def ready(at, i):
            for q in range(count + len(shared)):
                ref = piece(at, 1 - core, *(spans + twins)[q][:2])
                remote(ref, ref, sib_sems, (i, q), {"dp": sibling}).wait_recv()
            return at, i

        for q in range(count):
            for way in range(2):
                start(ring(way, 1, q))
        for q in range(count + len(shared)):
            start(across(chip, 0, q))
        after_start()
        behind = 2 if shared else 1
        for h in range(1, half + 1):
            todo = blocks(h - behind) if h >= behind else []
            for q in range(count):
                for way in range(2):
                    if not goes(way, h, q):
                        continue
                    at = chip_at(pos - h if way == 0 else pos + h)
                    ref = piece(at, core, *spans[q][:2])
                    remote(ref, ref, sems, (way, h - 1, q), {"dp": left}).wait_recv()
                    if goes(way, h + 1, q):
                        start(ring(way, h + 1, q))
                    if spans[q][3]:
                        start(over(at, number(way, h), shared.index(q)))
                    start(across(at, number(way, h), q))
                if q == (count - 1) // 2:
                    if h > 1:
                        from_twin(h - 1)
                    if todo:
                        work(*ready(*todo[0]))
                if q == count - 1 and len(todo) > 1:
                    work(*ready(*todo[1]))
        if shared:
            for at, i in blocks(half - 1):
                work(*ready(at, i))
            from_twin(half)
        ready(*blocks(half)[0])

    tile = 512

    merged[...] = jnp.broadcast_to(bias_ref[...], merged.shape)

    def merge(at, i):
        @pl.loop(0, width // tile)
        def _(j):
            cols = pl.ds(pl.multiple_of(j * tile, tile), tile)
            merged[:, cols] += jnp.dot(act[at], wbuf[at, :, cols], preferred_element_type=F32)

    def prepare():
        for copy in loads[1:]:
            copy.start()
        for t in range(chips):
            value = input_ref[:, t * 2 * depth : (t + 1) * 2 * depth].astype(F32)
            act[t] = (0.5 * value * (1.0 + lax.erf(value * 0.5**0.5))).astype(BF16)

    spans, twins = cut_up(W_PLAN if paired else X_PLAN, width, group)
    spans.append((None, None, 0, 0))
    gather(wbuf, depth, spans, twins, w_sems, w_sib, w_twin, merge, prepare)
    far = chip_at(pos + half)
    merge(far, 0)

    value = merged[...]
    scale = lax.rsqrt(jnp.mean(value * value, axis=1, keepdims=True) + 1e-06)
    mine = pl.ds(core * rows, rows)
    xbuf[chip, mine, :] = (value * scale * gain_ref[...]).astype(BF16)

    theirs = pl.ds((1 - core) * rows, rows)

    def swap(at, i):
        return remote(part.at[at, theirs, :], sib.at[at], r_sib, (i,), {"dp": sibling})

    hid_tile = 256

    def by_row(at, c, picked):
        table = cbuf[at, pl.ds(c * n, n), :]
        sums = lax.dot_general(table, picked, (((0,), (0,)), ((), ())), preferred_element_type=F32)
        return sums[:rows, :1]

    def expert(at, i):
        @pl.loop(0, hidden // hid_tile)
        def _(j):
            cols = pl.ds(pl.multiple_of(j * hid_tile, hid_tile), hid_tile)
            block = xbuf[at]
            gate = jnp.dot(block, gate_v[:, cols], preferred_element_type=F32)
            up = jnp.dot(block, up_v[:, cols], preferred_element_type=F32)
            hid[:, cols] = (jax.nn.silu(gate) * up).astype(BF16)

        picked = (lax.broadcasted_iota(jnp.int32, (n, LANES), 0) == me).astype(F32).astype(BF16)
        factor = jnp.concatenate([by_row(at, 0, picked), by_row(at, 1, picked)], axis=0)

        @pl.loop(0, width // tile)
        def _(j):
            cols = pl.ds(pl.multiple_of(j * tile, tile), tile)
            result = jnp.dot(hid[...], down_v[:, cols], preferred_element_type=F32).astype(BF16)
            part[at, :, cols] = (result.astype(F32) * factor).astype(BF16)

        start(swap(at, i))

    def wait_experts():
        for copy in loads[1:]:
            copy.wait()

    spans, _ = cut_up(X_PLAN, width, group)
    gather(xbuf, rows, spans, [], x_sems, x_sib, None, expert, wait_experts)

    cut = width // 2

    def span(q):
        return pl.ds(q * cut, cut)

    def landing(way, k):
        return (from_left if way == 0 else from_right).at[k - 1]

    def returned(way, k, q):
        dist = half + 1 - k
        at = chip_at(pos + dist if way == 0 else pos - dist)
        return remote(
            part.at[at, mine, span(q)],
            landing(way, k).at[:, span(q)],
            r_sems,
            (way, k - 1, q),
            {"dp": right if way == 0 else left},
        )

    def swapped(at, i):
        ref = sib.at[at]
        remote(ref, ref, r_sib, (i,), {"dp": sibling}).wait_recv()

    def landed(way, k, q):
        ref = landing(way, k).at[:, span(q)]
        remote(ref, ref, r_sems, (way, k - 1, q), {"dp": left}).wait_recv()

    def both(at, q):
        return part[at, mine, span(q)].astype(F32) + sib[at, :, span(q)].astype(F32)

    def send(way, k, q, more):
        dist = half + 1 - k
        at = chip_at(pos + dist if way == 0 else pos - dist)
        total = both(at, q)
        if more:
            landed(way, k - 1, q)
            total = total + landing(way, k - 1)[:, span(q)].astype(F32)
        part[at, mine, span(q)] = total.astype(BF16)
        start(returned(way, k, q))

    for way in range(2):
        d = half - 1
        at = chip_at(pos + d if way == 0 else pos - d)
        swapped(at, d + (1 - way) * (half - 1))
        send(way, 2, 1 - way, False)
    expert(far, 2 * half - 1)
    swapped(far, 2 * half - 1)
    for way in range(2):
        send(way, 1, way, False)
    for k in range(2, half + 1):
        dist = half + 1 - k
        if k > 2:
            for way in range(2):
                at = chip_at(pos + dist if way == 0 else pos - dist)
                swapped(at, dist + (1 - way) * (half - 1))
            for way in range(2):
                send(way, k, 1 - way, True)
        for way in range(2):
            send(way, k, way, True)
    swapped(chip, 0)
    inverse = 1.0 / by_row(chip, core, jnp.ones((n, LANES), BF16))
    for q in range(2):
        total = both(chip, q)
        for way in range(2):
            landed(way, half, q)
            total = total + landing(way, half)[:, span(q)].astype(F32)
        out_ref[:, span(q)] = (merged[:, span(q)] + total * inverse).astype(BF16)
    for copy in sent:
        copy.wait_send()


def fused_shards(
    merger_input,
    merger_weight,
    merger_bias,
    norm_gain,
    gate_weight,
    up_weight,
    down_weight,
    expert_ids,
    combine_ints,
):
    n = lax.axis_size("dp")
    chips, half = n // 2, n // 4
    rows = merger_input.shape[0]
    paired = lax.axis_size("groups") == 2
    depth, width = merger_weight.shape
    hidden = gate_weight.shape[2]
    vmem = pl.BlockSpec(memory_space=pltpu.VMEM)
    hbm = pl.BlockSpec(memory_space=pl.ANY)
    dma = pltpu.SemaphoreType.DMA
    return pl.pallas_call(
        functools.partial(fused_kernel, n, paired),
        out_shape=jax.ShapeDtypeStruct((rows, width), BF16),
        in_specs=[vmem] * 5 + [hbm] * 4,
        out_specs=vmem,
        scratch_shapes=[
            pltpu.VMEM((chips, rows, 2 * depth), BF16),
            pltpu.VMEM((chips, 2 * n, LANES), BF16),
            pltpu.VMEM((chips, 2 * depth, width), BF16),
            pltpu.VMEM((chips, 2 * rows, width), BF16),
            pltpu.VMEM((chips, 2 * rows, width), BF16),
            pltpu.VMEM((chips, rows, width), BF16),
            pltpu.VMEM((half, rows, width), BF16),
            pltpu.VMEM((half, rows, width), BF16),
            pltpu.VMEM((width, hidden), BF16),
            pltpu.VMEM((width, hidden), BF16),
            pltpu.VMEM((hidden, width), BF16),
            pltpu.VMEM((rows, width), F32),
            pltpu.VMEM((2 * rows, hidden), BF16),
            dma((4,)),
            dma((2, 2, half, max(len(W_PLAN), len(X_PLAN)) + 1)),
            dma((2, chips, 2 * len(W_PLAN) + len(X_PLAN) + 1)),
            dma((2, chips, len(W_PLAN))),
            dma((2, 2, half, len(X_PLAN))),
            dma((2, chips, len(X_PLAN))),
            dma((2, 2, half, 2)),
            dma((2, chips)),
        ],
        compiler_params=pltpu.CompilerParams(
            collective_id=0, has_side_effects=True, vmem_limit_bytes=VMEM_BYTES
        ),
    )(
        merger_input,
        expert_ids.T,
        combine_ints.T,
        merger_bias[None, :],
        norm_gain[None, :],
        merger_weight,
        gate_weight,
        up_weight,
        down_weight,
    )


def fits(n, rows, depth, width, hidden, local):
    if n % 4 or n < 8 or n > LANES or n % 16 or local != 1 or rows % 16 or rows >= LANES or depth % 16:
        return False
    if width % 2048 or hidden % 256:
        return False
    gathered = n * (depth * width + rows * width + n * LANES)
    sums = n * rows * width * 2 + n * rows * width // 2
    rest = 3 * width * hidden + 2 * rows * (hidden + width) + n * rows * depth
    return 2 * (gathered + sums + rest) < VMEM_BYTES - (8 << 20)


def shards(
    merger_input,
    merger_weight,
    merger_bias,
    norm_gain,
    gate_weight,
    up_weight,
    down_weight,
    expert_ids,
    combine_ints,
):
    n = lax.axis_size("dp")
    rows = merger_input.shape[0]
    depth, width = merger_weight.shape
    local, _, hidden = gate_weight.shape
    weights = (merger_weight, merger_bias, norm_gain, gate_weight, up_weight, down_weight)
    if fits(n, rows, depth, width, hidden, local):
        return fused_shards(merger_input, *weights, expert_ids, combine_ints)
    act = jax.nn.gelu(merger_input.astype(F32), approximate=False).astype(BF16)
    return routed_shards(act, *weights, expert_ids, combine_ints)


def solution(mesh):
    placed = (
        P(("groups", "dp"), None),
        P("dp", None),
        P(),
        P(),
        P("dp", None, None),
        P("dp", None, None),
        P("dp", None, None),
        P(("groups", "dp"), None),
        P(("groups", "dp"), None),
    )
    return jax.shard_map(
        shards, mesh=mesh, in_specs=placed, out_specs=P(("groups", "dp"), None), check_vma=False
    )
```
